32 devices in a mesh: seq: 4 (over y, x), mp: 8 (over z, core).
Axes of the slice: x: 2, y: 2, z: 4, core: 2. Of those that a mesh axis runs over, the one named last changes fastest.
Arguments:
- audio_feats: bfloat16 [16384, 512], P(('seq', 'mp')), may hold values from -6 to 6
- conv_first: bfloat16 [3, 3, 512, 256], replicated, may hold values from -0.15625 to 0.15625
- conv_second: bfloat16 [3, 256, 512], replicated, may hold values from -0.375 to 0.375
- down_weight: bfloat16 [16, 512, 512], replicated, may hold values from -0.09375 to 0.09375
- in_proj: bfloat16 [512, 4096], replicated, may hold values from -0.25 to 0.25
- norm_gain: float32 [4096], replicated, may hold values from 0.25 to 1.75
- qkv_weight: bfloat16 [3, 4096, 2048], P(None, None, 'mp'), may hold values from -0.09375 to 0.09375
- out_weight: bfloat16 [2048, 4096], P('mp'), may hold values from -0.125 to 0.125
Outputs:
- layer_out: bfloat16 [2048, 4096], P(('seq', 'mp'))
The draws below stay inside these ranges and needn't reach their ends.
All inputs are finite; a program needn't handle non-finite values.
Results may differ from the reference program's by a relative error of at most 0.023.
Values may be sent and summed in bfloat16 or wider, within the bound.
A program may use at most 128 MiB of HBM per device.

```python
import jax
import jax.numpy as jnp
from jax import lax

D = 4096
HEADS = 16
HD = 128
INNER = 2048
CH = 512
HALF = 256
STRIDE = 8
KSIZE = 16
STEPS = 16384
N_MP = 8


def draw_qkv_weight(key, part):
    inner = HEADS * HD
    scale = D ** (-0.5)
    keys = jax.random.split(key, 1)
    return (jnp.clip(jax.random.normal(keys[0], (3, D, inner), jnp.float32), -6.0, 6.0) * scale).astype(jnp.bfloat16)


def block_scale(key, extent, cuts, least, high):
    factor_of = 1.0
    for position, shards_of in cuts:
        steps = jax.random.uniform(jax.random.fold_in(jax.random.fold_in(key, 6), position), (shards_of,), jnp.float32, least / len(cuts), high / len(cuts))
        factor_of = factor_of * jnp.repeat(jnp.exp(steps), extent[position] // shards_of).reshape((-1,) + (1,) * (len(extent) - 1 - position))
    return factor_of


def noise(stream_key, extent, spread, limit, pieces=(), held_as=jnp.bfloat16):
    values = spread * jax.random.normal(stream_key, extent, jnp.float32)
    if pieces:
        values = values * block_scale(stream_key, extent, pieces, -0.22, 0.18)
    return jnp.clip(values, -limit, limit).astype(held_as)


def setup_inputs(seed: int = 0) -> dict:
    streams_of = jax.random.split(jax.random.key(seed), 9)
    return {
        "audio_feats": noise(streams_of[0], (STEPS, CH), 1.0, 6.0, ((0, 32),)),
        "conv_first": noise(streams_of[1], (3, 3, CH, HALF), (3 * CH) ** -0.5, 0.15625),
        "conv_second": noise(streams_of[2], (3, HALF, CH), HALF ** -0.5, 0.375),
        "down_weight": noise(streams_of[3], (KSIZE, CH, CH), (KSIZE * CH // 2) ** -0.5, 0.09375),
        "in_proj": noise(streams_of[4], (CH, D), CH ** -0.5, 0.25),
        "norm_gain": jnp.clip(1.0 + 0.15 * jax.random.normal(streams_of[5], (D,), jnp.float32), 0.25, 1.75),
        "qkv_weight": draw_qkv_weight(jax.random.fold_in(streams_of[8], 71), 0),
        "out_weight": noise(streams_of[7], (INNER, D), INNER ** -0.5, 0.125, ((0, 8),)),
    }


def causal_conv(u, weights, dilation):
    count = u.shape[0]
    padded = jnp.pad(u, ((2 * dilation, 0), (0, 0)))
    total = jnp.dot(padded[0:count], weights[0], preferred_element_type=jnp.float32)
    total = total + jnp.dot(padded[dilation:dilation + count], weights[1], preferred_element_type=jnp.float32)
    total = total + jnp.dot(padded[2 * dilation:2 * dilation + count], weights[2], preferred_element_type=jnp.float32)
    return total

def residual_unit(state, first, second, dilation):
    act = jax.nn.elu(state.astype(jnp.float32)).astype(jnp.bfloat16)
    middle = causal_conv(act, first, dilation)
    inner = jax.nn.elu(middle).astype(jnp.bfloat16)
    return (state.astype(jnp.float32) + jnp.dot(inner, second, preferred_element_type=jnp.float32)).astype(jnp.bfloat16)

def attend_heads(heads_q, heads_k, heads_v):
    length = heads_q.shape[1]
    qblock = min(1024, length)
    scale = HD ** (-0.5)
    results = []
    for block in range(length // qblock):
        begin = block * qblock
        stop = begin + qblock
        qpos = begin + jnp.arange(qblock, dtype=jnp.int32)
        kpos = jnp.arange(stop, dtype=jnp.int32)
        mask = kpos[None, :] <= qpos[:, None]

        def one(trio):
            scores = jnp.dot(trio[0][begin:stop], trio[1][:stop].T, preferred_element_type=jnp.float32) * scale
            scores = jnp.where(mask, scores, -1e+30)
            peak = lax.optimization_barrier(jnp.max(scores, axis=1, keepdims=True))
            probs = jnp.where(mask, jnp.exp(scores - peak), 0.0)
            total = lax.optimization_barrier(jnp.sum(probs, axis=1, keepdims=True))
            mixed = jnp.dot(probs.astype(jnp.bfloat16), trio[2][:stop], preferred_element_type=jnp.float32)
            return mixed / total
        results.append(lax.map(one, (heads_q, heads_k, heads_v)))
    return jnp.concatenate(results, axis=1)

def reference(audio_feats, conv_first, conv_second, down_weight, in_proj, norm_gain, qkv_weight, out_weight):
    state = audio_feats
    for unit, dilation in enumerate((1, 3, 9)):
        state = residual_unit(state, conv_first[unit], conv_second[unit], dilation)
    act = jax.nn.elu(state.astype(jnp.float32)).astype(jnp.bfloat16)
    padded = jnp.pad(act, ((STRIDE, 0), (0, 0)))
    channels = act.shape[1]
    grouped = padded.reshape(-1, STRIDE * channels)
    taps = down_weight.reshape(2, STRIDE * channels, channels)
    latent = (jnp.dot(grouped[:-1], taps[0], preferred_element_type=jnp.float32) + jnp.dot(grouped[1:], taps[1], preferred_element_type=jnp.float32)).astype(jnp.bfloat16)
    frames = jnp.dot(latent, in_proj, preferred_element_type=jnp.float32).astype(jnp.bfloat16)
    wide = frames.astype(jnp.float32)
    normed = (wide * lax.rsqrt(lax.optimization_barrier(jnp.mean(wide * wide, axis=1, keepdims=True)) + 1e-05) * norm_gain).astype(jnp.bfloat16)
    query = jnp.dot(normed, qkv_weight[0], preferred_element_type=jnp.float32).astype(jnp.bfloat16)
    keys = jnp.dot(normed, qkv_weight[1], preferred_element_type=jnp.float32).astype(jnp.bfloat16)
    values = jnp.dot(normed, qkv_weight[2], preferred_element_type=jnp.float32).astype(jnp.bfloat16)
    length = query.shape[0]
    heads_q = query.reshape(length, HEADS, HD).transpose(1, 0, 2)
    heads_k = keys.reshape(length, HEADS, HD).transpose(1, 0, 2)
    heads_v = values.reshape(length, HEADS, HD).transpose(1, 0, 2)
    mixed = attend_heads(heads_q, heads_k, heads_v)
    attn = mixed.transpose(1, 0, 2).reshape(length, HEADS * HD).astype(jnp.bfloat16)
    group_width = attn.shape[1] // N_MP
    attn_groups = attn.reshape(length, N_MP, group_width).transpose(1, 0, 2)
    weight_groups = out_weight.reshape(N_MP, group_width, out_weight.shape[1])

    def add_group(total, pair):
        part = jnp.dot(pair[0], pair[1], preferred_element_type=jnp.float32)
        rounded = lax.optimization_barrier(part.astype(jnp.bfloat16))
        return (total + rounded.astype(jnp.float32), None)
    summed, _ = lax.scan(add_group, jnp.zeros((length, out_weight.shape[1]), jnp.float32), (attn_groups, weight_groups))
    return (wide + summed).astype(jnp.bfloat16)
```

```python
import jax
import jax.numpy as jnp
from jax import lax
from jax.sharding import PartitionSpec as P

HD = 128
STRIDE = 8


def from_behind(block, axis, distance):
    devices = range(lax.axis_size(axis))
    route = [(i - distance, i) for i in devices if i - distance in devices]
    return lax.ppermute(block, axis, route)


def unit_apply(extended, first, second, dilation):
    count = extended.shape[0] - 2 * dilation
    act = jax.nn.elu(extended.astype(jnp.float32)).astype(jnp.bfloat16)
    middle = jnp.dot(act[0:count], first[0], preferred_element_type=jnp.float32)
    middle = middle + jnp.dot(
        act[dilation : dilation + count], first[1], preferred_element_type=jnp.float32
    )
    middle = middle + jnp.dot(
        act[2 * dilation : 2 * dilation + count], first[2], preferred_element_type=jnp.float32
    )
    inner = jax.nn.elu(middle).astype(jnp.bfloat16)
    kept = extended[2 * dilation :].astype(jnp.float32)
    return (kept + jnp.dot(inner, second, preferred_element_type=jnp.float32)).astype(jnp.bfloat16)


def body(
    audio_feats, conv_first, conv_second, down_weight, in_proj, norm_gain, qkv_weight, out_weight
):
    dilations = (1, 3, 9)
    channels = audio_feats.shape[1]
    depth = 2 * sum(dilations) + STRIDE
    rows = audio_feats.shape[0]
    extended = jnp.concatenate(
        [from_behind(audio_feats[rows - depth :], ("seq", "mp"), 1), audio_feats], axis=0
    )
    for unit in range(3):
        extended = unit_apply(extended, conv_first[unit], conv_second[unit], dilations[unit])
    act = jax.nn.elu(extended.astype(jnp.float32)).astype(jnp.bfloat16)
    grouped = act.reshape(-1, STRIDE * channels)
    taps = down_weight.reshape(2, STRIDE * channels, channels)
    latent = (
        jnp.dot(grouped[:-1], taps[0], preferred_element_type=jnp.float32)
        + jnp.dot(grouped[1:], taps[1], preferred_element_type=jnp.float32)
    ).astype(jnp.bfloat16)
    frames_mine = jnp.dot(latent, in_proj, preferred_element_type=jnp.float32).astype(jnp.bfloat16)
    wide = frames_mine.astype(jnp.float32)
    inverse = lax.rsqrt(jnp.mean(wide * wide, axis=1, keepdims=True) + 1e-05)
    scaled = (latent.astype(jnp.float32) * inverse).astype(jnp.bfloat16)
    everyone = lax.all_gather(scaled, ("seq", "mp"), axis=0, tiled=True)
    gained = (in_proj.astype(jnp.float32) * norm_gain).astype(jnp.bfloat16)
    folded = [
        jnp.dot(gained, qkv_weight[index], preferred_element_type=jnp.float32).astype(jnp.bfloat16)
        for index in range(3)
    ]
    shard = everyone.shape[0] // lax.axis_size("seq")
    mine = lax.dynamic_slice_in_dim(everyone, lax.axis_index("seq") * shard, shard, 0)
    query, key_piece, value_piece = (
        jnp.dot(rows_of, weight, preferred_element_type=jnp.float32).astype(jnp.bfloat16)
        for rows_of, weight in zip((mine, everyone, everyone), folded)
    )
    length = query.shape[0]
    columns = query.shape[1]
    local_heads = columns // HD
    heads_q = query.reshape(length, local_heads, HD)
    q_start = lax.axis_index("seq") * length
    qpos = q_start + jnp.arange(length, dtype=jnp.int32)
    scale = HD ** (-0.5)
    init = (
        jnp.full((local_heads, length), -1e30, jnp.float32),
        jnp.zeros((local_heads, length), jnp.float32),
        jnp.zeros((local_heads, length, HD), jnp.float32),
    )
    carry = init
    start = jnp.int32(0)
    rows = key_piece.shape[0]
    nblock = max(1, rows // 1024)
    blen = rows // nblock
    for index in range(nblock):
        k_start = start + index * blen
        key_block = key_piece[index * blen : (index + 1) * blen].reshape(blen, local_heads, HD)
        value_block = value_piece[index * blen : (index + 1) * blen].reshape(blen, local_heads, HD)
        update_peak, update_total, update_accum = carry
        scores = (
            jnp.einsum("qhd,khd->hqk", heads_q, key_block, preferred_element_type=jnp.float32)
            * scale
        )
        kpos = k_start + jnp.arange(blen, dtype=jnp.int32)
        mask = (kpos[None, :] <= qpos[:, None])[None]
        scores = jnp.where(mask, scores, -1e30)
        fresh = jnp.maximum(update_peak, jnp.max(scores, axis=2))
        probs = jnp.where(mask, jnp.exp(scores - fresh[:, :, None]), 0.0)
        factor = jnp.exp(update_peak - fresh)
        update_total = update_total * factor + jnp.sum(probs, axis=2)
        mixed = jnp.einsum(
            "hqk,khd->hqd",
            probs.astype(jnp.bfloat16),
            value_block,
            preferred_element_type=jnp.float32,
        )
        carry = (fresh, update_total, update_accum * factor[:, :, None] + mixed)
    peak, total, accum = carry
    attn = (
        (accum / total[:, :, None]).transpose(1, 0, 2).reshape(length, columns).astype(jnp.bfloat16)
    )
    summed = lax.psum_scatter(
        jnp.dot(attn, out_weight, preferred_element_type=jnp.float32).astype(jnp.bfloat16),
        "mp",
        scatter_dimension=0,
        tiled=True,
    ).astype(jnp.float32)
    return (frames_mine.astype(jnp.float32) + summed).astype(jnp.bfloat16)


def solution(mesh):
    placed = (P(("seq", "mp"), None), P(), P(), P(), P(), P(), P(None, None, "mp"), P("mp", None))
    return jax.shard_map(
        body, mesh=mesh, in_specs=placed, out_specs=P(("seq", "mp"), None), check_vma=False
    )
```

```python
import functools

import jax
import jax.numpy as jnp
from jax import lax
from jax.experimental import pallas as pl
from jax.experimental.pallas import tpu as pltpu
from jax.sharding import PartitionSpec as P

HD = 128
STRIDE = 8
DILATIONS = (1, 3, 9)
HALO = -(-(2 * sum(DILATIONS) + STRIDE) // 16) * 16
MESH = pl.DeviceIdType.MESH
F32 = jnp.float32
BF16 = jnp.bfloat16


def dot(a, b):
    return jnp.dot(a, b, preferred_element_type=F32)


def elu(x):
    low = jnp.minimum(x, 0.0)
    near = low * (1.0 + low * (0.5 + low * (1.0 / 6.0)))
    return jnp.where(x > 0.0, x, jnp.where(low > -0.03, near, jnp.exp(low) - 1.0))


def front_kernel(
    n_seq,
    n_mp,
    audio,
    first_hbm,
    second_hbm,
    down_hbm,
    proj_hbm,
    gain,
    qkv_hbm,
    frames_out,
    attn_out,
    halo,
    first,
    second,
    down,
    proj,
    qkv,
    act,
    gath,
    folded,
    peak,
    total,
    accum,
    load_sem,
    halo_sem,
    send_sem,
    recv_sem,
):
    seq = lax.axis_index("seq")
    mp = lax.axis_index("mp")
    n_z = n_mp // 2
    z = mp // 2
    core = mp % 2
    twin = mp + 1 - 2 * core
    linear = seq * n_mp + mp
    count = n_seq * n_mp
    after = (linear + 1) % count
    before = (linear + count - 1) % count
    rows = audio.shape[0]
    frames = gath.shape[1]
    channels = gath.shape[2]
    columns = folded.shape[2]
    heads = columns // HD

    loads = [
        pltpu.make_async_copy(src, dst, load_sem.at[i])
        for i, (src, dst) in enumerate(
            (
                (first_hbm, first),
                (second_hbm, second),
                (down_hbm, down),
                (proj_hbm, proj),
                (qkv_hbm, qkv),
            )
        )
    ]
    for load in loads:
        load.start()

    def z_peer(j):
        return (seq, ((z + j) % n_z) * 2 + core)

    def seq_peer(j):
        return ((seq + j) % n_seq, mp)

    barrier = pltpu.get_barrier_semaphore()
    peers = [z_peer(j) for j in range(1, n_z)] + [seq_peer(j) for j in range(1, n_seq)]
    peers += [(seq, twin), (after // n_mp, after % n_mp), (before // n_mp, before % n_mp)]
    for peer in peers:
        pl.semaphore_signal(barrier, inc=1, device_id=peer, device_id_type=MESH)
    pl.semaphore_wait(barrier, len(peers))

    edge = pltpu.make_async_remote_copy(
        src_ref=audio.at[pl.ds(rows - HALO, HALO)],
        dst_ref=halo,
        send_sem=halo_sem.at[0],
        recv_sem=halo_sem.at[1],
        device_id=(after // n_mp, after % n_mp),
        device_id_type=MESH,
    )
    edge.start()
    edge.wait_recv()
    behind = jnp.where(linear == 0, 0.0, halo[...].astype(F32))
    state = jnp.concatenate([behind, audio[...].astype(F32)], axis=0)
    for unit, dilation in enumerate(DILATIONS):
        u = elu(state).astype(BF16)
        if unit == 0:
            loads[0].wait()
        middle = dot(u, first[unit, 2])
        middle = middle + pltpu.roll(dot(u, first[unit, 1]), dilation, 0)
        middle = middle + pltpu.roll(dot(u, first[unit, 0]), 2 * dilation, 0)
        v = elu(middle).astype(BF16)
        if unit == 0:
            loads[1].wait()
        state = (state + dot(v, second[unit])).astype(BF16).astype(F32)
    act[...] = elu(state)[HALO - STRIDE :].reshape(act.shape)
    loads[2].wait()
    latent = jnp.zeros((frames, channels), F32)
    for tap in range(2 * STRIDE):
        begin = tap // STRIDE
        piece = act[begin : begin + frames, tap % STRIDE, :].astype(BF16)
        latent = latent + dot(piece, down[tap])
    latent = latent.astype(BF16)
    loads[3].wait()
    wide = dot(latent, proj[...]).astype(BF16)
    frames_out[...] = wide
    wide = wide.astype(F32)
    inverse = lax.rsqrt(jnp.mean(wide * wide, axis=1, keepdims=True) + 1e-05)
    gath[linear] = (latent.astype(F32) * inverse).astype(BF16)

    def send(slot, row, column, device):
        return pltpu.make_async_remote_copy(
            src_ref=gath.at[slot],
            dst_ref=gath.at[slot],
            send_sem=send_sem.at[row, column],
            recv_sem=recv_sem.at[slot],
            device_id=device,
            device_id_type=MESH,
        )

    sent = []

    def begin_send(*args):
        copy = send(*args)
        copy.start()
        sent.append(copy)

    def arrived(slot):
        send(slot, 0, 0, (seq, twin)).wait_recv()

    for j in range(1, n_z):
        begin_send(linear, 0, n_seq + j, z_peer(j))
    for j in range(1, n_seq):
        begin_send(linear, 0, j, seq_peer(j))
    begin_send(linear, 0, 0, (seq, twin))

    loads[4].wait()
    folded[...] = jnp.zeros_like(folded)
    depth = qkv.shape[1]
    step = 512

    def fold(index, carry):
        at = pl.ds(pl.multiple_of(index * step, step), step)
        gained = (proj[:, at].astype(F32) * gain[:, at]).astype(BF16)
        for part in range(3):
            folded[part] += dot(gained, qkv[part, at, :])
        return carry

    lax.fori_loop(0, depth // step, fold, 0)

    for i in range(1, n_z):
        slot = seq * n_mp + ((z + n_z - i) % n_z) * 2 + core
        arrived(slot)
        for j in range(1, n_seq):
            begin_send(slot, i, j, seq_peer(j))
        begin_send(slot, i, 0, (seq, twin))
    for j in range(1, n_seq):
        for i in range(n_z):
            slot = ((seq + n_seq - j) % n_seq) * n_mp + ((z + n_z - i) % n_z) * 2 + core
            arrived(slot)
            begin_send(slot, j * n_z + i, 0, (seq, twin))
    for j in range(n_seq):
        for i in range(n_z):
            slot = ((seq + n_seq - j) % n_seq) * n_mp + ((z + n_z - i) % n_z) * 2 + 1 - core
            arrived(slot)

    length = n_mp * frames
    w_q = (folded[0] * HD ** (-0.5)).astype(BF16)
    w_k = folded[1].astype(BF16)
    w_v = folded[2].astype(BF16)

    def block(index):
        at = pl.ds(pl.multiple_of(index * n_mp, n_mp), n_mp)
        return gath[at].reshape(length, channels)

    query = dot(block(seq), w_q).astype(BF16)
    peak[...] = jnp.full_like(peak, -1e30)
    total[...] = jnp.zeros_like(total)
    accum[...] = jnp.zeros_like(accum)

    def attend(index, diagonal):
        source = block(index)
        keys = dot(source, w_k).astype(BF16)
        values = dot(source, w_v).astype(BF16)
        for head in range(heads):
            at = slice(head * HD, (head + 1) * HD)
            scores = lax.dot_general(
                query[:, at], keys[:, at], (((1,), (1,)), ((), ())), preferred_element_type=F32
            )
            if diagonal:
                q_pos = lax.broadcasted_iota(jnp.int32, scores.shape, 0)
                k_pos = lax.broadcasted_iota(jnp.int32, scores.shape, 1)
                scores = jnp.where(k_pos <= q_pos, scores, -1e30)
            old = peak[head]
            fresh = jnp.maximum(old, jnp.max(scores, axis=1, keepdims=True))
            probs = jnp.exp(scores - fresh)
            factor = jnp.exp(old - fresh)
            peak[head] = fresh
            total[head] = total[head] * factor + jnp.sum(probs, axis=1, keepdims=True)
            accum[head] = accum[head] * factor + dot(probs.astype(BF16), values[:, at])

    attend(seq, True)

    def earlier(index, carry):
        attend(index, False)
        return carry

    lax.fori_loop(0, seq, earlier, 0)
    for head in range(heads):
        attn_out[:, head * HD : (head + 1) * HD] = (accum[head] / total[head]).astype(BF16)

    edge.wait_send()
    for copy in sent:
        copy.wait_send()


def front(n_seq, n_mp, audio, first, second, down, proj, gain, qkv):
    rows, channels = audio.shape
    frames = rows // STRIDE
    width = proj.shape[1]
    columns = qkv.shape[2]
    heads = columns // HD
    length = frames * n_mp
    n_z = n_mp // 2
    vmem = pl.BlockSpec(memory_space=pltpu.VMEM)
    hbm = pl.BlockSpec(memory_space=pl.ANY)
    flops = 2 * channels * width * columns * 3 + 12 * rows * channels * channels
    return pl.pallas_call(
        functools.partial(front_kernel, n_seq, n_mp),
        out_shape=(
            jax.ShapeDtypeStruct((frames, width), BF16),
            jax.ShapeDtypeStruct((length, columns), BF16),
        ),
        in_specs=[vmem, hbm, hbm, hbm, hbm, vmem, hbm],
        out_specs=(vmem, vmem),
        scratch_shapes=[
            pltpu.VMEM((HALO, channels), BF16),
            pltpu.VMEM(first.shape, BF16),
            pltpu.VMEM(second.shape, BF16),
            pltpu.VMEM(down.shape, BF16),
            pltpu.VMEM(proj.shape, BF16),
            pltpu.VMEM(qkv.shape, BF16),
            pltpu.VMEM((frames + 1, STRIDE, channels), F32),
            pltpu.VMEM((n_seq * n_mp, frames, channels), BF16),
            pltpu.VMEM((3, channels, columns), F32),
            pltpu.VMEM((heads, length, 1), F32),
            pltpu.VMEM((heads, length, 1), F32),
            pltpu.VMEM((heads, length, HD), F32),
            pltpu.SemaphoreType.DMA((5,)),
            pltpu.SemaphoreType.DMA((2,)),
            pltpu.SemaphoreType.DMA((n_seq * n_z, n_seq + n_z)),
            pltpu.SemaphoreType.DMA((n_seq * n_mp,)),
        ],
        compiler_params=pltpu.CompilerParams(
            collective_id=0, has_side_effects=True, vmem_limit_bytes=56 * 2**20
        ),
        cost_estimate=pl.CostEstimate(flops=flops, bytes_accessed=24 * 2**20, transcendentals=0),
    )(audio, first, second, down, proj, gain, qkv)


def body(
    n_seq,
    n_mp,
    audio_feats,
    conv_first,
    conv_second,
    down_weight,
    in_proj,
    norm_gain,
    qkv_weight,
    out_weight,
):
    frames_mine, attn = front(
        n_seq,
        n_mp,
        audio_feats,
        conv_first,
        conv_second,
        down_weight,
        in_proj,
        norm_gain.reshape(1, -1),
        qkv_weight,
    )
    summed = lax.psum_scatter(
        dot(attn, out_weight).astype(BF16), "mp", scatter_dimension=0, tiled=True
    ).astype(F32)
    return (frames_mine.astype(F32) + summed).astype(BF16)


def solution(mesh):
    placed = (P(("seq", "mp"), None), P(), P(), P(), P(), P(), P(None, None, "mp"), P("mp", None))
    return jax.shard_map(
        functools.partial(body, mesh.shape["seq"], mesh.shape["mp"]),
        mesh=mesh,
        in_specs=placed,
        out_specs=P(("seq", "mp"), None),
        check_vma=False,
    )
```

```python
import functools

import jax
import jax.numpy as jnp
from jax import lax
from jax.experimental import pallas as pl
from jax.experimental.pallas import tpu as pltpu
from jax.sharding import PartitionSpec as P

HD = 128
STRIDE = 8
DILATIONS = (1, 3, 9)
HALO = -(-(2 * sum(DILATIONS) + STRIDE) // 16) * 16
CHUNKS = 4
MESH = pl.DeviceIdType.MESH
F32 = jnp.float32
BF16 = jnp.bfloat16


def dot(a, b):
    return jnp.dot(a, b, preferred_element_type=F32)


def elu(x):
    low = jnp.minimum(x, 0.0)
    near = low * (1.0 + low * (0.5 + low * (1.0 / 6.0)))
    return jnp.where(x > 0.0, x, jnp.where(low > -0.03, near, jnp.exp(low) - 1.0))


def layer_kernel(
    n_seq,
    n_mp,
    audio,
    first_hbm,
    second_hbm,
    down_hbm,
    proj_hbm,
    gain,
    qkv_hbm,
    out_hbm,
    result,
    halo,
    first,
    second,
    down,
    proj,
    qkv,
    act,
    gath,
    folded,
    peak,
    total,
    accum,
    frames_mine,
    frames_sum,
    out_own,
    out_twin,
    out_pair,
    attn_own,
    attn_twin,
    attn_pair,
    leaving,
    coming,
    load_sem,
    halo_sem,
    send_sem,
    recv_sem,
    swap_send,
    swap_recv,
    chain_send,
    chain_recv,
):
    seq = lax.axis_index("seq")
    mp = lax.axis_index("mp")
    n_z = n_mp // 2
    z = mp // 2
    core = mp % 2
    twin = mp + 1 - 2 * core
    linear = seq * n_mp + mp
    count = n_seq * n_mp
    after = (linear + 1) % count
    before = (linear + count - 1) % count
    rows = audio.shape[0]
    frames = gath.shape[1]
    channels = gath.shape[2]
    columns = folded.shape[2]
    heads = columns // HD

    loads = [
        pltpu.make_async_copy(src, dst, load_sem.at[i])
        for i, (src, dst) in enumerate(
            (
                (first_hbm, first),
                (second_hbm, second),
                (down_hbm, down),
                (proj_hbm, proj),
                (qkv_hbm, qkv),
                (out_hbm, out_own),
            )
        )
    ]
    for load in loads:
        load.start()

    def z_peer(j):
        return (seq, ((z + j) % n_z) * 2 + core)

    def seq_peer(j):
        return ((seq + j) % n_seq, mp)

    barrier = pltpu.get_barrier_semaphore()
    peers = [z_peer(j) for j in range(1, n_z)] + [seq_peer(j) for j in range(1, n_seq)]
    pair = z + 1 - 2 * (z % 2)
    pair_same = (seq, pair * 2 + core)
    pair_other = (seq, pair * 2 + 1 - core)
    peers += [(seq, twin), pair_other, (after // n_mp, after % n_mp), (before // n_mp, before % n_mp)]
    for peer in peers:
        pl.semaphore_signal(barrier, inc=1, device_id=peer, device_id_type=MESH)
    pl.semaphore_wait(barrier, len(peers))

    edge = pltpu.make_async_remote_copy(
        src_ref=audio.at[pl.ds(rows - HALO, HALO)],
        dst_ref=halo,
        send_sem=halo_sem.at[0],
        recv_sem=halo_sem.at[1],
        device_id=(after // n_mp, after % n_mp),
        device_id_type=MESH,
    )
    edge.start()

    def swap(index, src, dst, device):
        return pltpu.make_async_remote_copy(
            src_ref=src,
            dst_ref=dst,
            send_sem=swap_send.at[index],
            recv_sem=swap_recv.at[index],
            device_id=device,
            device_id_type=MESH,
        )

    paired_width = out_pair.shape[2]
    weight_swaps = [
        swap(0, out_hbm, out_twin, (seq, twin)),
        swap(
            1,
            out_hbm.at[:, pl.ds(out_hbm.shape[1] - paired_width, paired_width)],
            out_pair.at[core],
            pair_same,
        ),
    ]
    for copy in weight_swaps:
        copy.start()
    edge.wait_recv()
    behind = jnp.where(linear == 0, 0.0, halo[...].astype(F32))
    state = jnp.concatenate([behind, audio[...].astype(F32)], axis=0)
    for unit, dilation in enumerate(DILATIONS):
        u = elu(state).astype(BF16)
        if unit == 0:
            loads[0].wait()
        middle = dot(u, first[unit, 2])
        middle = middle + pltpu.roll(dot(u, first[unit, 1]), dilation, 0)
        middle = middle + pltpu.roll(dot(u, first[unit, 0]), 2 * dilation, 0)
        v = elu(middle).astype(BF16)
        if unit == 0:
            loads[1].wait()
        state = (state + dot(v, second[unit])).astype(BF16).astype(F32)
    act[...] = elu(state)[HALO - STRIDE :].reshape(act.shape)
    loads[2].wait()
    latent = jnp.zeros((frames, channels), F32)
    for tap in range(2 * STRIDE):
        begin = tap // STRIDE
        piece = act[begin : begin + frames, tap % STRIDE, :].astype(BF16)
        latent = latent + dot(piece, down[tap])
    latent = latent.astype(BF16)
    loads[3].wait()
    wide = dot(latent, proj[...]).astype(BF16)
    frames_mine[...] = wide
    wide = wide.astype(F32)
    inverse = lax.rsqrt(jnp.mean(wide * wide, axis=1, keepdims=True) + 1e-05)
    gath[linear] = (latent.astype(F32) * inverse).astype(BF16)

    def send(slot, row, column, device):
        return pltpu.make_async_remote_copy(
            src_ref=gath.at[slot],
            dst_ref=gath.at[slot],
            send_sem=send_sem.at[row, column],
            recv_sem=recv_sem.at[slot],
            device_id=device,
            device_id_type=MESH,
        )

    sent = []

    def begin_send(*args):
        copy = send(*args)
        copy.start()
        sent.append(copy)

    def arrived(slot):
        send(slot, 0, 0, (seq, twin)).wait_recv()

    for j in range(1, n_z):
        begin_send(linear, 0, n_seq + j, z_peer(j))
    for j in range(1, n_seq):
        begin_send(linear, 0, j, seq_peer(j))
    begin_send(linear, 0, 0, (seq, twin))

    loads[4].wait()
    folded[...] = jnp.zeros_like(folded)
    depth = qkv.shape[1]
    step = 512

    def fold(index, carry):
        at = pl.ds(pl.multiple_of(index * step, step), step)
        gained = (proj[:, at].astype(F32) * gain[:, at]).astype(BF16)
        for part in range(3):
            folded[part] += dot(gained, qkv[part, at, :])
        return carry

    lax.fori_loop(0, depth // step, fold, 0)

    for i in range(1, n_z):
        slot = seq * n_mp + ((z + n_z - i) % n_z) * 2 + core
        arrived(slot)
        for j in range(1, n_seq):
            begin_send(slot, i, j, seq_peer(j))
        begin_send(slot, i, 0, (seq, twin))
    for j in range(1, n_seq):
        for i in range(n_z):
            slot = ((seq + n_seq - j) % n_seq) * n_mp + ((z + n_z - i) % n_z) * 2 + core
            arrived(slot)
            begin_send(slot, j * n_z + i, 0, (seq, twin))
    for j in range(n_seq):
        for i in range(n_z):
            slot = ((seq + n_seq - j) % n_seq) * n_mp + ((z + n_z - i) % n_z) * 2 + 1 - core
            arrived(slot)

    weight_swaps[1].wait_recv()
    passed = swap(2, out_pair.at[core], out_pair.at[core], (seq, twin))
    passed.start()

    length = n_mp * frames
    w_q = (folded[0] * HD ** (-0.5)).astype(BF16)
    w_k = folded[1].astype(BF16)
    w_v = folded[2].astype(BF16)

    def block(index):
        at = pl.ds(pl.multiple_of(index * n_mp, n_mp), n_mp)
        return gath[at].reshape(length, channels)

    query = dot(block(seq), w_q).astype(BF16)
    peak[...] = jnp.full_like(peak, -1e30)
    total[...] = jnp.zeros_like(total)
    accum[...] = jnp.zeros_like(accum)

    def attend(index, diagonal):
        source = block(index)
        keys = dot(source, w_k).astype(BF16)
        values = dot(source, w_v).astype(BF16)
        for head in range(heads):
            at = slice(head * HD, (head + 1) * HD)
            scores = lax.dot_general(
                query[:, at], keys[:, at], (((1,), (1,)), ((), ())), preferred_element_type=F32
            )
            if diagonal:
                q_pos = lax.broadcasted_iota(jnp.int32, scores.shape, 0)
                k_pos = lax.broadcasted_iota(jnp.int32, scores.shape, 1)
                scores = jnp.where(k_pos <= q_pos, scores, -1e30)
            old = peak[head]
            fresh = jnp.maximum(old, jnp.max(scores, axis=1, keepdims=True))
            probs = jnp.exp(scores - fresh)
            factor = jnp.exp(old - fresh)
            peak[head] = fresh
            total[head] = total[head] * factor + jnp.sum(probs, axis=1, keepdims=True)
            accum[head] = accum[head] * factor + dot(probs.astype(BF16), values[:, at])

    attend(seq, True)

    def earlier(index, carry):
        attend(index, False)
        return carry

    lax.fori_loop(0, seq, earlier, 0)
    for head in range(heads):
        at = slice(head * HD, (head + 1) * HD)
        mixed = (accum[head] / total[head]).astype(BF16).reshape(n_z, 2, frames, HD)
        for side in range(2):
            attn_own[side, :, :, at] = mixed[:, side]

    attn_swaps = [swap(3, attn_own.at[1 - core], attn_twin, (seq, twin))]
    for side in range(2):
        attn_swaps.append(
            pltpu.make_async_remote_copy(
                src_ref=attn_own.at[side],
                dst_ref=attn_pair.at[core],
                send_sem=swap_send.at[4 + side],
                recv_sem=swap_recv.at[4 + core],
                device_id=(seq, pair * 2 + side),
                device_id_type=MESH,
            )
        )
    for copy in attn_swaps:
        copy.start()
    loads[5].wait()
    weight_swaps[0].wait_recv()
    passed.wait_recv()
    attn_swaps[0].wait_recv()

    chunks = leaving.shape[1]
    width = leaving.shape[3]
    plain = chunks - paired_width // width

    def partial(dest, chunk):
        at = slice(chunk * width, (chunk + 1) * width)
        value = dot(attn_own[core, dest], out_own[:, at]) + dot(attn_twin[dest], out_twin[:, at])
        if chunk >= plain:
            at = slice((chunk - plain) * width, (chunk - plain + 1) * width)
            for side in range(2):
                value = value + dot(attn_pair[side, dest], out_pair[side, :, at])
        return value

    def hop(way, dest, chunk, device):
        return pltpu.make_async_remote_copy(
            src_ref=leaving.at[dest, chunk],
            dst_ref=coming.at[way, dest, chunk],
            send_sem=chain_send.at[dest, chunk],
            recv_sem=chain_recv.at[way, dest, chunk],
            device_id=(seq, device * 2 + core),
            device_id_type=MESH,
        )

    def plan(way, dest, chunk):
        odd = z % 2 == 1
        if way == 0:
            if chunk < plain:
                return z < dest, z > 0, jnp.minimum(z + 1, n_z - 1)
            return jnp.logical_and(z < dest, odd), z >= 2, jnp.minimum(z + 2, dest)
        if chunk < plain:
            return z > dest, z < n_z - 1, jnp.maximum(z - 1, 0)
        return (
            jnp.logical_and(z > dest, jnp.logical_not(odd)),
            z < n_z - 2,
            jnp.maximum(z - 2, dest),
        )

    order = [(k, chunk) for k in range(1, n_z) for chunk in range(chunks)]
    for k, chunk in order:
        if k == 1 and chunk == plain:
            for side in range(2):
                swap(4 + side, attn_own.at[0], attn_pair.at[side], pair_same).wait_recv()
        for way, dest in ((0, n_z - k), (1, k - 1)):
            active, has, device = plan(way, dest, chunk)

            @pl.when(active)
            def _(way=way, dest=dest, chunk=chunk, has=has, device=device):
                value = partial(dest, chunk)

                @pl.when(has)
                def _():
                    hop(way, dest, chunk, pair).wait_recv()
                    leaving[dest, chunk] = (
                        value + coming[way, dest, chunk].astype(F32)
                    ).astype(BF16)

                @pl.when(jnp.logical_not(has))
                def _():
                    leaving[dest, chunk] = value.astype(BF16)

                hop(way, dest, chunk, device).start()

    for chunk in range(chunks):
        at = slice(chunk * width, (chunk + 1) * width)
        accum_out = frames_mine[:, at].astype(F32) + partial(z, chunk)
        frames_sum[:, at] = accum_out
    for chunk in range(chunks):
        at = slice(chunk * width, (chunk + 1) * width)
        edges = (z > 0, z < n_z - 1) if chunk < plain else (z >= 2, z < n_z - 2)
        for way in range(2):

            @pl.when(edges[way])
            def _(way=way, chunk=chunk, at=at):
                hop(way, z, chunk, pair).wait_recv()
                frames_sum[:, at] += coming[way, z, chunk].astype(F32)

        result[:, at] = frames_sum[:, at].astype(BF16)

    edge.wait_send()
    for copy in sent + weight_swaps + [passed] + attn_swaps:
        copy.wait_send()
    for k, chunk in order:
        for way, dest in ((0, n_z - k), (1, k - 1)):
            active, has, device = plan(way, dest, chunk)

            @pl.when(active)
            def _(way=way, dest=dest, chunk=chunk, device=device):
                hop(way, dest, chunk, device).wait_send()


def layer(n_seq, n_mp, audio, first, second, down, proj, gain, qkv, out):
    rows, channels = audio.shape
    frames = rows // STRIDE
    width = proj.shape[1]
    columns = qkv.shape[2]
    heads = columns // HD
    length = frames * n_mp
    n_z = n_mp // 2
    vmem = pl.BlockSpec(memory_space=pltpu.VMEM)
    hbm = pl.BlockSpec(memory_space=pl.ANY)
    flops = 2 * channels * width * columns * 3 + 12 * rows * channels * channels
    return pl.pallas_call(
        functools.partial(layer_kernel, n_seq, n_mp),
        out_shape=jax.ShapeDtypeStruct((frames, width), BF16),
        in_specs=[vmem, hbm, hbm, hbm, hbm, vmem, hbm, hbm],
        out_specs=vmem,
        scratch_shapes=[
            pltpu.VMEM((HALO, channels), BF16),
            pltpu.VMEM(first.shape, BF16),
            pltpu.VMEM(second.shape, BF16),
            pltpu.VMEM(down.shape, BF16),
            pltpu.VMEM(proj.shape, BF16),
            pltpu.VMEM(qkv.shape, BF16),
            pltpu.VMEM((frames + 1, STRIDE, channels), F32),
            pltpu.VMEM((n_seq * n_mp, frames, channels), BF16),
            pltpu.VMEM((3, channels, columns), F32),
            pltpu.VMEM((heads, length, 1), F32),
            pltpu.VMEM((heads, length, 1), F32),
            pltpu.VMEM((heads, length, HD), F32),
            pltpu.VMEM((frames, width), BF16),
            pltpu.VMEM((frames, width), F32),
            pltpu.VMEM(out.shape, BF16),
            pltpu.VMEM(out.shape, BF16),
            pltpu.VMEM((2, columns, width // 2), BF16),
            pltpu.VMEM((2, n_z, frames, columns), BF16),
            pltpu.VMEM((n_z, frames, columns), BF16),
            pltpu.VMEM((2, n_z, frames, columns), BF16),
            pltpu.VMEM((n_z, CHUNKS, frames, width // CHUNKS), BF16),
            pltpu.VMEM((2, n_z, CHUNKS, frames, width // CHUNKS), BF16),
            pltpu.SemaphoreType.DMA((6,)),
            pltpu.SemaphoreType.DMA((2,)),
            pltpu.SemaphoreType.DMA((n_seq * n_z, n_seq + n_z)),
            pltpu.SemaphoreType.DMA((n_seq * n_mp,)),
            pltpu.SemaphoreType.DMA((6,)),
            pltpu.SemaphoreType.DMA((6,)),
            pltpu.SemaphoreType.DMA((n_z, CHUNKS)),
            pltpu.SemaphoreType.DMA((2, n_z, CHUNKS)),
        ],
        compiler_params=pltpu.CompilerParams(
            collective_id=0, has_side_effects=True, vmem_limit_bytes=60 * 2**20
        ),
        cost_estimate=pl.CostEstimate(flops=flops, bytes_accessed=24 * 2**20, transcendentals=0),
    )(audio, first, second, down, proj, gain, qkv, out)


def body(
    n_seq,
    n_mp,
    audio_feats,
    conv_first,
    conv_second,
    down_weight,
    in_proj,
    norm_gain,
    qkv_weight,
    out_weight,
):
    return layer(
        n_seq,
        n_mp,
        audio_feats,
        conv_first,
        conv_second,
        down_weight,
        in_proj,
        norm_gain.reshape(1, -1),
        qkv_weight,
        out_weight,
    )


def solution(mesh):
    placed = (P(("seq", "mp"), None), P(), P(), P(), P(), P(), P(None, None, "mp"), P("mp", None))
    return jax.shard_map(
        functools.partial(body, mesh.shape["seq"], mesh.shape["mp"]),
        mesh=mesh,
        in_specs=placed,
        out_specs=P(("seq", "mp"), None),
        check_vma=False,
    )
```

```python
import functools

import jax
import jax.numpy as jnp
from jax import lax
from jax.experimental import pallas as pl
from jax.experimental.pallas import tpu as pltpu
from jax.sharding import PartitionSpec as P

HD = 128
STRIDE = 8
DILATIONS = (1, 3, 9)
HALO = -(-(2 * sum(DILATIONS) + STRIDE) // 16) * 16
CHUNKS = 4
MESH = pl.DeviceIdType.MESH
F32 = jnp.float32
BF16 = jnp.bfloat16


def dot(a, b):
    return jnp.dot(a, b, preferred_element_type=F32)


def elu(x):
    low = jnp.minimum(x, 0.0)
    near = low * (1.0 + low * (0.5 + low * (1.0 / 6.0)))
    return jnp.where(x > 0.0, x, jnp.where(low > -0.03, near, jnp.exp(low) - 1.0))


def layer_kernel(
    n_seq,
    n_mp,
    audio,
    first_hbm,
    second_hbm,
    down_hbm,
    proj_hbm,
    gain,
    qkv_hbm,
    out_hbm,
    result,
    halo,
    first,
    second,
    down,
    proj,
    qkv,
    act,
    gath,
    folded,
    peak,
    total,
    accum,
    frames_mine,
    frames_sum,
    out_own,
    out_twin,
    out_pair,
    attn_own,
    attn_twin,
    attn_pair,
    leaving,
    coming,
    load_sem,
    halo_sem,
    send_sem,
    recv_sem,
    swap_send,
    swap_recv,
    chain_send,
    chain_recv,
):
    seq = lax.axis_index("seq")
    mp = lax.axis_index("mp")
    n_z = n_mp // 2
    z = mp // 2
    core = mp % 2
    twin = mp + 1 - 2 * core
    linear = seq * n_mp + mp
    count = n_seq * n_mp
    after = (linear + 1) % count
    before = (linear + count - 1) % count
    rows = audio.shape[0]
    frames = gath.shape[1]
    channels = gath.shape[2]
    columns = folded.shape[2]
    heads = columns // HD

    loads = [
        pltpu.make_async_copy(src, dst, load_sem.at[i])
        for i, (src, dst) in enumerate(
            (
                (first_hbm, first),
                (second_hbm, second),
                (down_hbm, down),
                (proj_hbm, proj),
                (qkv_hbm, qkv),
                (out_hbm, out_own),
            )
        )
    ]
    for load in loads:
        load.start()

    def z_peer(j):
        return (seq, ((z + j) % n_z) * 2 + core)

    def seq_peer(j):
        return ((seq + j) % n_seq, mp)

    barrier = pltpu.get_barrier_semaphore()
    peers = [z_peer(j) for j in range(1, n_z)] + [seq_peer(j) for j in range(1, n_seq)]
    pair = z + 1 - 2 * (z % 2)
    pair_same = (seq, pair * 2 + core)
    pair_other = (seq, pair * 2 + 1 - core)
    peers += [(seq, twin), pair_other, (after // n_mp, after % n_mp), (before // n_mp, before % n_mp)]
    for peer in peers:
        pl.semaphore_signal(barrier, inc=1, device_id=peer, device_id_type=MESH)
    pl.semaphore_wait(barrier, len(peers))

    edge = pltpu.make_async_remote_copy(
        src_ref=audio.at[pl.ds(rows - HALO, HALO)],
        dst_ref=halo,
        send_sem=halo_sem.at[0],
        recv_sem=halo_sem.at[1],
        device_id=(after // n_mp, after % n_mp),
        device_id_type=MESH,
    )
    edge.start()

    def swap(index, src, dst, device):
        return pltpu.make_async_remote_copy(
            src_ref=src,
            dst_ref=dst,
            send_sem=swap_send.at[index],
            recv_sem=swap_recv.at[index],
            device_id=device,
            device_id_type=MESH,
        )

    paired_width = out_pair.shape[2]
    weight_swaps = [
        swap(0, out_hbm, out_twin, (seq, twin)),
        swap(
            1,
            out_hbm.at[:, pl.ds(out_hbm.shape[1] - paired_width, paired_width)],
            out_pair.at[core],
            pair_same,
        ),
    ]
    for copy in weight_swaps:
        copy.start()
    edge.wait_recv()
    behind = jnp.where(linear == 0, 0.0, halo[...].astype(F32))
    state = jnp.concatenate([behind, audio[...].astype(F32)], axis=0)
    for unit, dilation in enumerate(DILATIONS):
        u = elu(state).astype(BF16)
        if unit == 0:
            loads[0].wait()
        middle = dot(u, first[unit, 2])
        middle = middle + pltpu.roll(dot(u, first[unit, 1]), dilation, 0)
        middle = middle + pltpu.roll(dot(u, first[unit, 0]), 2 * dilation, 0)
        v = elu(middle).astype(BF16)
        if unit == 0:
            loads[1].wait()
        state = (state + dot(v, second[unit])).astype(BF16).astype(F32)
    act[...] = elu(state)[HALO - STRIDE :].reshape(act.shape)
    loads[2].wait()
    latent = jnp.zeros((frames, channels), F32)
    for tap in range(2 * STRIDE):
        begin = tap // STRIDE
        piece = act[begin : begin + frames, tap % STRIDE, :].astype(BF16)
        latent = latent + dot(piece, down[tap])
    latent = latent.astype(BF16)
    loads[3].wait()
    wide = dot(latent, proj[...]).astype(BF16)
    frames_mine[...] = wide
    wide = wide.astype(F32)
    inverse = lax.rsqrt(jnp.mean(wide * wide, axis=1, keepdims=True) + 1e-05)
    gath[linear] = (latent.astype(F32) * inverse).astype(BF16)

    def send(slot, row, column, device):
        return pltpu.make_async_remote_copy(
            src_ref=gath.at[slot],
            dst_ref=gath.at[slot],
            send_sem=send_sem.at[row, column],
            recv_sem=recv_sem.at[slot],
            device_id=device,
            device_id_type=MESH,
        )

    sent = []

    def begin_send(*args):
        copy = send(*args)
        copy.start()
        sent.append(copy)

    def arrived(slot):
        send(slot, 0, 0, (seq, twin)).wait_recv()

    for j in range(1, n_z):
        begin_send(linear, 0, n_seq + j, z_peer(j))
    for j in range(1, n_seq):
        begin_send(linear, 0, j, seq_peer(j))
    begin_send(linear, 0, 0, (seq, twin))

    loads[4].wait()
    folded[...] = jnp.zeros_like(folded)
    depth = qkv.shape[1]
    step = 512

    def fold(index, carry):
        at = pl.ds(pl.multiple_of(index * step, step), step)
        gained = (proj[:, at].astype(F32) * gain[:, at]).astype(BF16)
        for part in range(3):
            folded[part] += dot(gained, qkv[part, at, :])
        return carry

    lax.fori_loop(0, depth // step, fold, 0)

    for i in range(1, n_z):
        slot = seq * n_mp + ((z + n_z - i) % n_z) * 2 + core
        arrived(slot)
        for j in range(1, n_seq):
            begin_send(slot, i, j, seq_peer(j))
        begin_send(slot, i, 0, (seq, twin))
    for j in range(1, n_seq):
        for i in range(n_z):
            slot = ((seq + n_seq - j) % n_seq) * n_mp + ((z + n_z - i) % n_z) * 2 + core
            arrived(slot)
            begin_send(slot, j * n_z + i, 0, (seq, twin))
    for j in range(n_seq):
        for i in range(n_z):
            slot = ((seq + n_seq - j) % n_seq) * n_mp + ((z + n_z - i) % n_z) * 2 + 1 - core
            arrived(slot)

    weight_swaps[1].wait_recv()
    passed = swap(2, out_pair.at[core], out_pair.at[core], (seq, twin))
    passed.start()

    length = n_mp * frames
    w_q = (folded[0] * HD ** (-0.5)).astype(BF16)
    w_k = folded[1].astype(BF16)
    w_v = folded[2].astype(BF16)

    def block(index):
        at = pl.ds(pl.multiple_of(index * n_mp, n_mp), n_mp)
        return gath[at].reshape(length, channels)

    query = dot(block(seq), w_q).astype(BF16)
    peak[...] = jnp.full_like(peak, -1e30)
    total[...] = jnp.zeros_like(total)
    accum[...] = jnp.zeros_like(accum)

    def attend(index, diagonal):
        source = block(index)
        keys = dot(source, w_k).astype(BF16)
        values = dot(source, w_v).astype(BF16)
        for head in range(heads):
            at = slice(head * HD, (head + 1) * HD)
            scores = lax.dot_general(
                query[:, at], keys[:, at], (((1,), (1,)), ((), ())), preferred_element_type=F32
            )
            if diagonal:
                q_pos = lax.broadcasted_iota(jnp.int32, scores.shape, 0)
                k_pos = lax.broadcasted_iota(jnp.int32, scores.shape, 1)
                scores = jnp.where(k_pos <= q_pos, scores, -1e30)
            old = peak[head]
            fresh = jnp.maximum(old, jnp.max(scores, axis=1, keepdims=True))
            probs = jnp.exp(scores - fresh)
            factor = jnp.exp(old - fresh)
            peak[head] = fresh
            total[head] = total[head] * factor + jnp.sum(probs, axis=1, keepdims=True)
            accum[head] = accum[head] * factor + dot(probs.astype(BF16), values[:, at])

    attend(seq, True)

    def earlier(index, carry):
        attend(index, False)
        return carry

    lax.fori_loop(0, seq, earlier, 0)
    for head in range(heads):
        at = slice(head * HD, (head + 1) * HD)
        mixed = (accum[head] / total[head]).astype(BF16).reshape(n_z, 2, frames, HD)
        for side in range(2):
            attn_own[side, :, :, at] = mixed[:, side]

    attn_swaps = [swap(3, attn_own.at[1 - core], attn_twin, (seq, twin))]
    for side in range(2):
        attn_swaps.append(
            pltpu.make_async_remote_copy(
                src_ref=attn_own.at[side],
                dst_ref=attn_pair.at[core],
                send_sem=swap_send.at[4 + side],
                recv_sem=swap_recv.at[4 + core],
                device_id=(seq, pair * 2 + side),
                device_id_type=MESH,
            )
        )
    for copy in attn_swaps:
        copy.start()
    loads[5].wait()
    weight_swaps[0].wait_recv()
    passed.wait_recv()
    attn_swaps[0].wait_recv()

    chunks = leaving.shape[1]
    width = leaving.shape[3]
    plain = chunks - paired_width // width

    def whole(ref):
        return ref[...].reshape(n_z * frames, columns)

    def multiply(chunk):
        at = slice(chunk * width, (chunk + 1) * width)
        value = dot(attn_own[core].reshape(n_z * frames, columns), out_own[:, at])
        value = value + dot(whole(attn_twin), out_twin[:, at])
        if chunk >= plain:
            at = slice((chunk - plain) * width, (chunk - plain + 1) * width)
            for side in range(2):
                value = value + dot(whole(attn_pair.at[side]), out_pair[side, :, at])
        leaving[:, chunk] = value.astype(BF16).reshape(n_z, frames, width)

    def hop(way, dest, chunk, device):
        return pltpu.make_async_remote_copy(
            src_ref=leaving.at[dest, chunk],
            dst_ref=coming.at[way, dest, chunk],
            send_sem=chain_send.at[dest, chunk],
            recv_sem=chain_recv.at[way, dest, chunk],
            device_id=(seq, device * 2 + core),
            device_id_type=MESH,
        )

    last = n_z - 1
    odd = z % 2
    near = jnp.where(z < n_z // 2, 0, 1)

    def plan(phase, k, chunk):
        way = near if phase == 0 else 1 - near
        dest = jnp.where(way == 0, n_z - k, k - 1)
        ahead = jnp.where(way == 0, dest - z, z - dest)
        passed_by = jnp.where(way == 0, z, last - z)
        if chunk < plain:
            active, has, stride = ahead > 0, passed_by > 0, 1
        else:
            inner = jnp.where(way == 0, odd, 1 - odd)
            active, has = jnp.logical_and(ahead > 0, inner == 1), passed_by >= 2
            stride = jnp.clip(ahead, 0, 2)
        device = jnp.clip(jnp.where(way == 0, z + stride, z - stride), 0, last)
        return way, dest, active, has, device

    order = [(p, k, c) for p in range(2) for k in range(1, n_z) for c in range(chunks)]
    for phase, k, chunk in order:
        if phase == 0 and k == 1:
            if chunk == plain:
                for side in range(2):
                    swap(4 + side, attn_own.at[0], attn_pair.at[side], pair_same).wait_recv()
            multiply(chunk)
        way, dest, active, has, device = plan(phase, k, chunk)

        @pl.when(jnp.logical_and(active, has))
        def _(way=way, dest=dest, chunk=chunk):
            hop(way, dest, chunk, pair).wait_recv()
            leaving[dest, chunk] = (
                leaving[dest, chunk].astype(F32) + coming[way, dest, chunk].astype(F32)
            ).astype(BF16)

        @pl.when(active)
        def _(way=way, dest=dest, chunk=chunk, device=device):
            hop(way, dest, chunk, device).start()

    for chunk in range(chunks):
        at = slice(chunk * width, (chunk + 1) * width)
        frames_sum[:, at] = frames_mine[:, at].astype(F32) + leaving[z, chunk].astype(F32)
        edges = (z > 0, z < last) if chunk < plain else (z >= 2, z < last - 1)
        for way in range(2):

            @pl.when(edges[way])
            def _(way=way, chunk=chunk, at=at):
                hop(way, z, chunk, pair).wait_recv()
                frames_sum[:, at] += coming[way, z, chunk].astype(F32)

        result[:, at] = frames_sum[:, at].astype(BF16)

    edge.wait_send()
    for copy in sent + weight_swaps + [passed] + attn_swaps:
        copy.wait_send()
    for phase, k, chunk in order:
        way, dest, active, has, device = plan(phase, k, chunk)

        @pl.when(active)
        def _(way=way, dest=dest, chunk=chunk, device=device):
            hop(way, dest, chunk, device).wait_send()


def layer(n_seq, n_mp, audio, first, second, down, proj, gain, qkv, out):
    rows, channels = audio.shape
    frames = rows // STRIDE
    width = proj.shape[1]
    columns = qkv.shape[2]
    heads = columns // HD
    length = frames * n_mp
    n_z = n_mp // 2
    vmem = pl.BlockSpec(memory_space=pltpu.VMEM)
    hbm = pl.BlockSpec(memory_space=pl.ANY)
    flops = 2 * channels * width * columns * 3 + 12 * rows * channels * channels
    return pl.pallas_call(
        functools.partial(layer_kernel, n_seq, n_mp),
        out_shape=jax.ShapeDtypeStruct((frames, width), BF16),
        in_specs=[vmem, hbm, hbm, hbm, hbm, vmem, hbm, hbm],
        out_specs=vmem,
        scratch_shapes=[
            pltpu.VMEM((HALO, channels), BF16),
            pltpu.VMEM(first.shape, BF16),
            pltpu.VMEM(second.shape, BF16),
            pltpu.VMEM(down.shape, BF16),
            pltpu.VMEM(proj.shape, BF16),
            pltpu.VMEM(qkv.shape, BF16),
            pltpu.VMEM((frames + 1, STRIDE, channels), F32),
            pltpu.VMEM((n_seq * n_mp, frames, channels), BF16),
            pltpu.VMEM((3, channels, columns), F32),
            pltpu.VMEM((heads, length, 1), F32),
            pltpu.VMEM((heads, length, 1), F32),
            pltpu.VMEM((heads, length, HD), F32),
            pltpu.VMEM((frames, width), BF16),
            pltpu.VMEM((frames, width), F32),
            pltpu.VMEM(out.shape, BF16),
            pltpu.VMEM(out.shape, BF16),
            pltpu.VMEM((2, columns, width // 2), BF16),
            pltpu.VMEM((2, n_z, frames, columns), BF16),
            pltpu.VMEM((n_z, frames, columns), BF16),
            pltpu.VMEM((2, n_z, frames, columns), BF16),
            pltpu.VMEM((n_z, CHUNKS, frames, width // CHUNKS), BF16),
            pltpu.VMEM((2, n_z, CHUNKS, frames, width // CHUNKS), BF16),
            pltpu.SemaphoreType.DMA((6,)),
            pltpu.SemaphoreType.DMA((2,)),
            pltpu.SemaphoreType.DMA((n_seq * n_z, n_seq + n_z)),
            pltpu.SemaphoreType.DMA((n_seq * n_mp,)),
            pltpu.SemaphoreType.DMA((6,)),
            pltpu.SemaphoreType.DMA((6,)),
            pltpu.SemaphoreType.DMA((n_z, CHUNKS)),
            pltpu.SemaphoreType.DMA((2, n_z, CHUNKS)),
        ],
        compiler_params=pltpu.CompilerParams(
            collective_id=0, has_side_effects=True, vmem_limit_bytes=60 * 2**20
        ),
        cost_estimate=pl.CostEstimate(flops=flops, bytes_accessed=24 * 2**20, transcendentals=0),
    )(audio, first, second, down, proj, gain, qkv, out)


def body(
    n_seq,
    n_mp,
    audio_feats,
    conv_first,
    conv_second,
    down_weight,
    in_proj,
    norm_gain,
    qkv_weight,
    out_weight,
):
    return layer(
        n_seq,
        n_mp,
        audio_feats,
        conv_first,
        conv_second,
        down_weight,
        in_proj,
        norm_gain.reshape(1, -1),
        qkv_weight,
        out_weight,
    )


def solution(mesh):
    placed = (P(("seq", "mp"), None), P(), P(), P(), P(), P(), P(None, None, "mp"), P("mp", None))
    return jax.shard_map(
        functools.partial(body, mesh.shape["seq"], mesh.shape["mp"]),
        mesh=mesh,
        in_specs=placed,
        out_specs=P(("seq", "mp"), None),
        check_vma=False,
    )
```

```python
import functools

import jax
import jax.numpy as jnp
from jax import lax
from jax.experimental import pallas as pl
from jax.experimental.pallas import tpu as pltpu
from jax.sharding import PartitionSpec as P

HD = 128
STRIDE = 8
DILATIONS = (1, 3, 9)
HALO = -(-(2 * sum(DILATIONS) + STRIDE) // 16) * 16
CHUNKS = 4
MESH = pl.DeviceIdType.MESH
F32 = jnp.float32
BF16 = jnp.bfloat16


def dot(a, b):
    return jnp.dot(a, b, preferred_element_type=F32)


def elu(x):
    low = jnp.minimum(x, 0.0)
    near = low * (1.0 + low * (0.5 + low * (1.0 / 6.0)))
    return jnp.where(x > 0.0, x, jnp.where(low > -0.03, near, jnp.exp(low) - 1.0))


def layer_kernel(
    n_seq,
    n_mp,
    audio,
    first_hbm,
    second_hbm,
    down_hbm,
    proj_hbm,
    gain,
    qkv_hbm,
    out_hbm,
    result,
    halo,
    first,
    second,
    down,
    proj,
    qkv,
    act,
    gath,
    folded,
    peak,
    total,
    accum,
    frames_mine,
    frames_sum,
    out_own,
    out_twin,
    out_pair,
    attn_own,
    attn_twin,
    attn_pair,
    leaving,
    coming,
    load_sem,
    halo_sem,
    send_sem,
    recv_sem,
    swap_send,
    swap_recv,
    chain_send,
    chain_recv,
):
    seq = lax.axis_index("seq")
    mp = lax.axis_index("mp")
    n_z = n_mp // 2
    z = mp // 2
    core = mp % 2
    twin = mp + 1 - 2 * core
    linear = seq * n_mp + mp
    count = n_seq * n_mp
    after = (linear + 1) % count
    before = (linear + count - 1) % count
    rows = audio.shape[0]
    frames = gath.shape[1]
    channels = gath.shape[2]
    columns = folded.shape[2]
    heads = columns // HD

    loads = [
        pltpu.make_async_copy(src, dst, load_sem.at[i])
        for i, (src, dst) in enumerate(
            (
                (first_hbm, first),
                (second_hbm, second),
                (down_hbm, down),
                (proj_hbm, proj),
                (qkv_hbm, qkv),
                (out_hbm, out_own),
            )
        )
    ]
    for load in loads:
        load.start()

    def z_peer(j):
        return (seq, ((z + j) % n_z) * 2 + core)

    def seq_peer(j):
        return ((seq + j) % n_seq, mp)

    barrier = pltpu.get_barrier_semaphore()
    peers = [z_peer(j) for j in range(1, n_z)] + [seq_peer(j) for j in range(1, n_seq)]
    pair = z + 1 - 2 * (z % 2)
    pair_same = (seq, pair * 2 + core)
    pair_other = (seq, pair * 2 + 1 - core)
    peers += [(seq, twin), pair_other, (after // n_mp, after % n_mp), (before // n_mp, before % n_mp)]
    for peer in peers:
        pl.semaphore_signal(barrier, inc=1, device_id=peer, device_id_type=MESH)
    pl.semaphore_wait(barrier, len(peers))

    edge = pltpu.make_async_remote_copy(
        src_ref=audio.at[pl.ds(rows - HALO, HALO)],
        dst_ref=halo,
        send_sem=halo_sem.at[0],
        recv_sem=halo_sem.at[1],
        device_id=(after // n_mp, after % n_mp),
        device_id_type=MESH,
    )
    edge.start()

    def swap(index, src, dst, device):
        return pltpu.make_async_remote_copy(
            src_ref=src,
            dst_ref=dst,
            send_sem=swap_send.at[index],
            recv_sem=swap_recv.at[index],
            device_id=device,
            device_id_type=MESH,
        )

    paired_width = out_pair.shape[2]
    part = paired_width // 2

    def weight_part(index):
        begin = out_hbm.shape[1] - paired_width + index * part
        return swap(
            1 + index,
            out_hbm.at[:, pl.ds(begin, part)],
            out_pair.at[core, :, pl.ds(index * part, part)],
            pair_same,
        )

    def pass_part(index):
        here = out_pair.at[core, :, pl.ds(index * part, part)]
        return swap(6 + index, here, here, (seq, twin))

    weight_swaps = [swap(0, out_hbm, out_twin, (seq, twin)), weight_part(0)]
    for copy in weight_swaps:
        copy.start()
    edge.wait_recv()
    behind = jnp.where(linear == 0, 0.0, halo[...].astype(F32))
    state = jnp.concatenate([behind, audio[...].astype(F32)], axis=0)
    for unit, dilation in enumerate(DILATIONS):
        u = elu(state).astype(BF16)
        if unit == 0:
            loads[0].wait()
        middle = dot(u, first[unit, 2])
        middle = middle + pltpu.roll(dot(u, first[unit, 1]), dilation, 0)
        middle = middle + pltpu.roll(dot(u, first[unit, 0]), 2 * dilation, 0)
        v = elu(middle).astype(BF16)
        if unit == 0:
            loads[1].wait()
        state = (state + dot(v, second[unit])).astype(BF16).astype(F32)
    act[...] = elu(state)[HALO - STRIDE :].reshape(act.shape)
    loads[2].wait()
    latent = jnp.zeros((frames, channels), F32)
    for tap in range(2 * STRIDE):
        begin = tap // STRIDE
        piece = act[begin : begin + frames, tap % STRIDE, :].astype(BF16)
        latent = latent + dot(piece, down[tap])
    latent = latent.astype(BF16)
    loads[3].wait()
    wide = dot(latent, proj[...]).astype(BF16)
    frames_mine[...] = wide
    wide = wide.astype(F32)
    inverse = lax.rsqrt(jnp.mean(wide * wide, axis=1, keepdims=True) + 1e-05)
    gath[linear] = (latent.astype(F32) * inverse).astype(BF16)

    def send(slot, row, column, device):
        return pltpu.make_async_remote_copy(
            src_ref=gath.at[slot],
            dst_ref=gath.at[slot],
            send_sem=send_sem.at[row, column],
            recv_sem=recv_sem.at[slot],
            device_id=device,
            device_id_type=MESH,
        )

    sent = []

    def begin_send(*args):
        copy = send(*args)
        copy.start()
        sent.append(copy)

    def arrived(slot):
        send(slot, 0, 0, (seq, twin)).wait_recv()

    for j in range(1, n_z):
        begin_send(linear, 0, n_seq + j, z_peer(j))
    for j in range(1, n_seq):
        begin_send(linear, 0, j, seq_peer(j))
    begin_send(linear, 0, 0, (seq, twin))

    loads[4].wait()
    folded[...] = jnp.zeros_like(folded)
    depth = qkv.shape[1]
    step = 512

    def fold(index, carry):
        at = pl.ds(pl.multiple_of(index * step, step), step)
        gained = (proj[:, at].astype(F32) * gain[:, at]).astype(BF16)
        for part in range(3):
            folded[part] += dot(gained, qkv[part, at, :])
        return carry

    lax.fori_loop(0, depth // step, fold, 0)

    for i in range(1, n_z):
        slot = seq * n_mp + ((z + n_z - i) % n_z) * 2 + core
        arrived(slot)
        for j in range(1, n_seq):
            begin_send(slot, i, j, seq_peer(j))
        begin_send(slot, i, 0, (seq, twin))
    weight_swaps.append(weight_part(1))
    weight_swaps[2].start()

    length = n_mp * frames
    w_q = (folded[0] * HD ** (-0.5)).astype(BF16)
    w_k = folded[1].astype(BF16)
    w_v = folded[2].astype(BF16)

    def block(index):
        at = pl.ds(pl.multiple_of(index * n_mp, n_mp), n_mp)
        return gath[at].reshape(length, channels)

    peak[...] = jnp.full_like(peak, -1e30)
    total[...] = jnp.zeros_like(total)
    accum[...] = jnp.zeros_like(accum)

    def attend(query, index, diagonal):
        source = block(index)
        keys = dot(source, w_k).astype(BF16)
        values = dot(source, w_v).astype(BF16)
        for head in range(heads):
            at = slice(head * HD, (head + 1) * HD)
            scores = lax.dot_general(
                query[:, at], keys[:, at], (((1,), (1,)), ((), ())), preferred_element_type=F32
            )
            if diagonal:
                q_pos = lax.broadcasted_iota(jnp.int32, scores.shape, 0)
                k_pos = lax.broadcasted_iota(jnp.int32, scores.shape, 1)
                scores = jnp.where(k_pos <= q_pos, scores, -1e30)
            old = peak[head]
            fresh = jnp.maximum(old, jnp.max(scores, axis=1, keepdims=True))
            probs = jnp.exp(scores - fresh)
            factor = jnp.exp(old - fresh)
            peak[head] = fresh
            total[head] = total[head] * factor + jnp.sum(probs, axis=1, keepdims=True)
            accum[head] = accum[head] * factor + dot(probs.astype(BF16), values[:, at])

    passed = []
    for j in range(n_seq):
        source_seq = (seq + n_seq - j) % n_seq
        for i in range(n_z):
            slot = source_seq * n_mp + ((z + n_z - i) % n_z) * 2 + core
            if j > 0:
                arrived(slot)
                begin_send(slot, j * n_z + i, 0, (seq, twin))
        for i in range(n_z):
            arrived(source_seq * n_mp + ((z + n_z - i) % n_z) * 2 + 1 - core)
        if j < 2:
            weight_swaps[1 + j].wait_recv()
            passed.append(pass_part(j))
            passed[j].start()
        if j == 0:
            query = dot(block(seq), w_q).astype(BF16)
            attend(query, seq, True)
        else:

            @pl.when(seq >= j)
            def _(j=j):
                attend(query, seq - j, False)

    for head in range(heads):
        at = slice(head * HD, (head + 1) * HD)
        mixed = (accum[head] / total[head]).astype(BF16).reshape(n_z, 2, frames, HD)
        for side in range(2):
            attn_own[side, :, :, at] = mixed[:, side]

    attn_swaps = [swap(3, attn_own.at[1 - core], attn_twin, (seq, twin))]
    for side in range(2):
        attn_swaps.append(
            pltpu.make_async_remote_copy(
                src_ref=attn_own.at[side],
                dst_ref=attn_pair.at[core],
                send_sem=swap_send.at[4 + side],
                recv_sem=swap_recv.at[4 + core],
                device_id=(seq, pair * 2 + side),
                device_id_type=MESH,
            )
        )
    for copy in attn_swaps:
        copy.start()
    loads[5].wait()
    weight_swaps[0].wait_recv()
    for copy in passed:
        copy.wait_recv()
    attn_swaps[0].wait_recv()

    chunks = leaving.shape[1]
    width = leaving.shape[3]
    plain = chunks - paired_width // width

    def whole(ref):
        return ref[...].reshape(n_z * frames, columns)

    def multiply(chunk):
        at = slice(chunk * width, (chunk + 1) * width)
        value = dot(attn_own[core].reshape(n_z * frames, columns), out_own[:, at])
        value = value + dot(whole(attn_twin), out_twin[:, at])
        if chunk >= plain:
            at = slice((chunk - plain) * width, (chunk - plain + 1) * width)
            for side in range(2):
                value = value + dot(whole(attn_pair.at[side]), out_pair[side, :, at])
        leaving[:, chunk] = value.astype(BF16).reshape(n_z, frames, width)

    def hop(way, dest, chunk, device):
        return pltpu.make_async_remote_copy(
            src_ref=leaving.at[dest, chunk],
            dst_ref=coming.at[way, dest, chunk],
            send_sem=chain_send.at[dest, chunk],
            recv_sem=chain_recv.at[way, dest, chunk],
            device_id=(seq, device * 2 + core),
            device_id_type=MESH,
        )

    last = n_z - 1
    odd = z % 2
    near = jnp.where(z < n_z // 2, 0, 1)

    def plan(phase, k, chunk):
        way = near if phase == 0 else 1 - near
        dest = jnp.where(way == 0, n_z - k, k - 1)
        ahead = jnp.where(way == 0, dest - z, z - dest)
        passed_by = jnp.where(way == 0, z, last - z)
        if chunk < plain:
            active, has, stride = ahead > 0, passed_by > 0, 1
        else:
            inner = jnp.where(way == 0, odd, 1 - odd)
            active, has = jnp.logical_and(ahead > 0, inner == 1), passed_by >= 2
            stride = jnp.clip(ahead, 0, 2)
        device = jnp.clip(jnp.where(way == 0, z + stride, z - stride), 0, last)
        return way, dest, active, has, device

    def settle(phase, k, chunk):
        way, dest, active, has, device = plan(phase, k, chunk)

        @pl.when(active)
        def _():
            hop(way, dest, chunk, device).wait_send()

    order = [(p, k, c) for p in range(2) for k in range(1, n_z) for c in range(chunks)]
    for phase, k, chunk in order:
        if phase == 0 and k == 1:
            if chunk == plain:
                for side in range(2):
                    swap(4 + side, attn_own.at[0], attn_pair.at[side], pair_same).wait_recv()
            multiply(chunk)
        way, dest, active, has, device = plan(phase, k, chunk)
        if k > 1:
            settle(phase, k - 1, chunk)

        @pl.when(jnp.logical_and(active, has))
        def _(way=way, dest=dest, chunk=chunk):
            hop(way, dest, chunk, pair).wait_recv()
            leaving[dest, chunk] = (
                leaving[dest, chunk].astype(F32) + coming[way, dest, chunk].astype(F32)
            ).astype(BF16)

        @pl.when(active)
        def _(way=way, dest=dest, chunk=chunk, device=device):
            hop(way, dest, chunk, device).start()

    for chunk in range(chunks):
        at = slice(chunk * width, (chunk + 1) * width)
        frames_sum[:, at] = frames_mine[:, at].astype(F32) + leaving[z, chunk].astype(F32)
        edges = (z > 0, z < last) if chunk < plain else (z >= 2, z < last - 1)
        for way in range(2):

            @pl.when(edges[way])
            def _(way=way, chunk=chunk, at=at):
                hop(way, z, chunk, pair).wait_recv()
                frames_sum[:, at] += coming[way, z, chunk].astype(F32)

        result[:, at] = frames_sum[:, at].astype(BF16)

    edge.wait_send()
    for copy in sent + weight_swaps + passed + attn_swaps:
        copy.wait_send()
    for phase in range(2):
        for chunk in range(chunks):
            settle(phase, last, chunk)


def layer(n_seq, n_mp, audio, first, second, down, proj, gain, qkv, out):
    rows, channels = audio.shape
    frames = rows // STRIDE
    width = proj.shape[1]
    columns = qkv.shape[2]
    heads = columns // HD
    length = frames * n_mp
    n_z = n_mp // 2
    vmem = pl.BlockSpec(memory_space=pltpu.VMEM)
    hbm = pl.BlockSpec(memory_space=pl.ANY)
    flops = 2 * channels * width * columns * 3 + 12 * rows * channels * channels
    return pl.pallas_call(
        functools.partial(layer_kernel, n_seq, n_mp),
        out_shape=jax.ShapeDtypeStruct((frames, width), BF16),
        in_specs=[vmem, hbm, hbm, hbm, hbm, vmem, hbm, hbm],
        out_specs=vmem,
        scratch_shapes=[
            pltpu.VMEM((HALO, channels), BF16),
            pltpu.VMEM(first.shape, BF16),
            pltpu.VMEM(second.shape, BF16),
            pltpu.VMEM(down.shape, BF16),
            pltpu.VMEM(proj.shape, BF16),
            pltpu.VMEM(qkv.shape, BF16),
            pltpu.VMEM((frames + 1, STRIDE, channels), F32),
            pltpu.VMEM((n_seq * n_mp, frames, channels), BF16),
            pltpu.VMEM((3, channels, columns), F32),
            pltpu.VMEM((heads, length, 1), F32),
            pltpu.VMEM((heads, length, 1), F32),
            pltpu.VMEM((heads, length, HD), F32),
            pltpu.VMEM((frames, width), BF16),
            pltpu.VMEM((frames, width), F32),
            pltpu.VMEM(out.shape, BF16),
            pltpu.VMEM(out.shape, BF16),
            pltpu.VMEM((2, columns, width // 2), BF16),
            pltpu.VMEM((2, n_z, frames, columns), BF16),
            pltpu.VMEM((n_z, frames, columns), BF16),
            pltpu.VMEM((2, n_z, frames, columns), BF16),
            pltpu.VMEM((n_z, CHUNKS, frames, width // CHUNKS), BF16),
            pltpu.VMEM((2, n_z, CHUNKS, frames, width // CHUNKS), BF16),
            pltpu.SemaphoreType.DMA((6,)),
            pltpu.SemaphoreType.DMA((2,)),
            pltpu.SemaphoreType.DMA((n_seq * n_z, n_seq + n_z)),
            pltpu.SemaphoreType.DMA((n_seq * n_mp,)),
            pltpu.SemaphoreType.DMA((8,)),
            pltpu.SemaphoreType.DMA((8,)),
            pltpu.SemaphoreType.DMA((n_z, CHUNKS)),
            pltpu.SemaphoreType.DMA((2, n_z, CHUNKS)),
        ],
        compiler_params=pltpu.CompilerParams(
            collective_id=0, has_side_effects=True, vmem_limit_bytes=60 * 2**20
        ),
        cost_estimate=pl.CostEstimate(flops=flops, bytes_accessed=24 * 2**20, transcendentals=0),
    )(audio, first, second, down, proj, gain, qkv, out)


def body(
    n_seq,
    n_mp,
    audio_feats,
    conv_first,
    conv_second,
    down_weight,
    in_proj,
    norm_gain,
    qkv_weight,
    out_weight,
):
    return layer(
        n_seq,
        n_mp,
        audio_feats,
        conv_first,
        conv_second,
        down_weight,
        in_proj,
        norm_gain.reshape(1, -1),
        qkv_weight,
        out_weight,
    )


def solution(mesh):
    placed = (P(("seq", "mp"), None), P(), P(), P(), P(), P(), P(None, None, "mp"), P("mp", None))
    return jax.shard_map(
        functools.partial(body, mesh.shape["seq"], mesh.shape["mp"]),
        mesh=mesh,
        in_specs=placed,
        out_specs=P(("seq", "mp"), None),
        check_vma=False,
    )
```

```python
import functools

import jax
import jax.numpy as jnp
from jax import lax
from jax.experimental import pallas as pl
from jax.experimental.pallas import tpu as pltpu
from jax.sharding import PartitionSpec as P

HD = 128
STRIDE = 8
DILATIONS = (1, 3, 9)
HALO = -(-(2 * sum(DILATIONS) + STRIDE) // 16) * 16
CHUNKS = 4
MESH = pl.DeviceIdType.MESH
F32 = jnp.float32
BF16 = jnp.bfloat16


def dot(a, b):
    return jnp.dot(a, b, preferred_element_type=F32)


def elu(x):
    low = jnp.minimum(x, 0.0)
    near = low * (1.0 + low * (0.5 + low * (1.0 / 6.0)))
    return jnp.where(x > 0.0, x, jnp.where(low > -0.03, near, jnp.exp(low) - 1.0))


def layer_kernel(
    n_seq,
    n_mp,
    audio,
    first_hbm,
    second_hbm,
    down_hbm,
    proj_hbm,
    gain,
    qkv_hbm,
    out_hbm,
    result,
    halo,
    first,
    second,
    down,
    proj,
    qkv,
    act,
    gath,
    folded,
    peak,
    total,
    accum,
    frames_mine,
    frames_sum,
    out_own,
    out_twin,
    out_pair,
    attn_own,
    attn_twin,
    attn_pair,
    leaving,
    coming,
    load_sem,
    halo_sem,
    send_sem,
    recv_sem,
    swap_send,
    swap_recv,
    chain_send,
    chain_recv,
):
    seq = lax.axis_index("seq")
    mp = lax.axis_index("mp")
    n_z = n_mp // 2
    z = mp // 2
    core = mp % 2
    twin = mp + 1 - 2 * core
    linear = seq * n_mp + mp
    count = n_seq * n_mp
    after = (linear + 1) % count
    before = (linear + count - 1) % count
    rows = audio.shape[0]
    frames = gath.shape[1]
    channels = gath.shape[2]
    columns = folded.shape[2]
    heads = columns // HD

    loads = [
        pltpu.make_async_copy(src, dst, load_sem.at[i])
        for i, (src, dst) in enumerate(
            (
                (first_hbm, first),
                (second_hbm, second),
                (down_hbm, down),
                (proj_hbm, proj),
                (qkv_hbm, qkv),
                (out_hbm, out_own),
            )
        )
    ]
    for load in loads:
        load.start()

    def z_peer(j):
        return (seq, ((z + j) % n_z) * 2 + core)

    def seq_peer(j):
        return ((seq + j) % n_seq, mp)

    barrier = pltpu.get_barrier_semaphore()
    peers = [z_peer(j) for j in range(1, n_z)] + [seq_peer(j) for j in range(1, n_seq)]
    pair = z + 1 - 2 * (z % 2)
    pair_same = (seq, pair * 2 + core)
    pair_other = (seq, pair * 2 + 1 - core)
    peers += [(seq, twin), pair_other, (after // n_mp, after % n_mp), (before // n_mp, before % n_mp)]
    for peer in peers:
        pl.semaphore_signal(barrier, inc=1, device_id=peer, device_id_type=MESH)
    pl.semaphore_wait(barrier, len(peers))

    edge = pltpu.make_async_remote_copy(
        src_ref=audio.at[pl.ds(rows - HALO, HALO)],
        dst_ref=halo,
        send_sem=halo_sem.at[0],
        recv_sem=halo_sem.at[1],
        device_id=(after // n_mp, after % n_mp),
        device_id_type=MESH,
    )
    edge.start()

    def swap(index, src, dst, device):
        return pltpu.make_async_remote_copy(
            src_ref=src,
            dst_ref=dst,
            send_sem=swap_send.at[index],
            recv_sem=swap_recv.at[index],
            device_id=device,
            device_id_type=MESH,
        )

    paired_width = out_pair.shape[2]
    part = paired_width // 2

    def weight_part(index):
        begin = out_hbm.shape[1] - paired_width + index * part
        return swap(
            1 + index,
            out_hbm.at[:, pl.ds(begin, part)],
            out_pair.at[core, :, pl.ds(index * part, part)],
            pair_same,
        )

    def pass_part(index):
        here = out_pair.at[core, :, pl.ds(index * part, part)]
        return swap(6 + index, here, here, (seq, twin))

    weight_swaps = [swap(0, out_hbm, out_twin, (seq, twin)), weight_part(0)]
    for copy in weight_swaps:
        copy.start()
    loads[0].wait()
    ready = elu(audio[...].astype(F32)).astype(BF16)
    ready = [dot(ready, first[0, tap]) for tap in range(3)]
    edge.wait_recv()
    behind = jnp.where(linear == 0, 0.0, halo[...].astype(F32))
    state = jnp.concatenate([behind, audio[...].astype(F32)], axis=0)
    for unit, dilation in enumerate(DILATIONS):
        u = elu(state[:HALO] if unit == 0 else state).astype(BF16)
        taps = [dot(u, first[unit, tap]) for tap in range(3)]
        if unit == 0:
            taps = [jnp.concatenate(both, axis=0) for both in zip(taps, ready)]
        middle = taps[2] + pltpu.roll(taps[1], dilation, 0)
        middle = middle + pltpu.roll(taps[0], 2 * dilation, 0)
        v = elu(middle).astype(BF16)
        if unit == 0:
            loads[1].wait()
        state = (state + dot(v, second[unit])).astype(BF16).astype(F32)
    act[...] = elu(state)[HALO - STRIDE :].reshape(act.shape)
    loads[2].wait()
    latent = jnp.zeros((frames, channels), F32)
    for tap in range(2 * STRIDE):
        begin = tap // STRIDE
        piece = act[begin : begin + frames, tap % STRIDE, :].astype(BF16)
        latent = latent + dot(piece, down[tap])
    latent = latent.astype(BF16)
    loads[3].wait()
    wide = dot(latent, proj[...]).astype(BF16)
    frames_mine[...] = wide
    wide = wide.astype(F32)
    inverse = lax.rsqrt(jnp.mean(wide * wide, axis=1, keepdims=True) + 1e-05)
    gath[linear] = (latent.astype(F32) * inverse).astype(BF16)

    def send(slot, row, column, device):
        return pltpu.make_async_remote_copy(
            src_ref=gath.at[slot],
            dst_ref=gath.at[slot],
            send_sem=send_sem.at[row, column],
            recv_sem=recv_sem.at[slot],
            device_id=device,
            device_id_type=MESH,
        )

    sent = []

    def begin_send(*args):
        copy = send(*args)
        copy.start()
        sent.append(copy)

    def arrived(slot):
        send(slot, 0, 0, (seq, twin)).wait_recv()

    for j in range(1, n_z):
        begin_send(linear, 0, n_seq + j, z_peer(j))
    for j in range(1, n_seq):
        begin_send(linear, 0, j, seq_peer(j))
    begin_send(linear, 0, 0, (seq, twin))

    loads[4].wait()
    folded[...] = jnp.zeros_like(folded)
    depth = qkv.shape[1]
    step = 512

    def fold(index, carry):
        at = pl.ds(pl.multiple_of(index * step, step), step)
        gained = (proj[:, at].astype(F32) * gain[:, at]).astype(BF16)
        for part in range(3):
            folded[part] += dot(gained, qkv[part, at, :])
        return carry

    lax.fori_loop(0, depth // step, fold, 0)

    for i in range(1, n_z):
        slot = seq * n_mp + ((z + n_z - i) % n_z) * 2 + core
        arrived(slot)
        for j in range(1, n_seq):
            begin_send(slot, i, j, seq_peer(j))
        begin_send(slot, i, 0, (seq, twin))
    weight_swaps.append(weight_part(1))
    weight_swaps[2].start()

    length = n_mp * frames
    w_q = (folded[0] * HD ** (-0.5)).astype(BF16)
    w_k = folded[1].astype(BF16)
    w_v = folded[2].astype(BF16)

    def block(index):
        at = pl.ds(pl.multiple_of(index * n_mp, n_mp), n_mp)
        return gath[at].reshape(length, channels)

    peak[...] = jnp.full_like(peak, -1e30)
    total[...] = jnp.zeros_like(total)
    accum[...] = jnp.zeros_like(accum)

    def attend(query, index, diagonal):
        source = block(index)
        keys = dot(source, w_k).astype(BF16)
        values = dot(source, w_v).astype(BF16)
        for head in range(heads):
            at = slice(head * HD, (head + 1) * HD)
            scores = lax.dot_general(
                query[:, at], keys[:, at], (((1,), (1,)), ((), ())), preferred_element_type=F32
            )
            if diagonal:
                q_pos = lax.broadcasted_iota(jnp.int32, scores.shape, 0)
                k_pos = lax.broadcasted_iota(jnp.int32, scores.shape, 1)
                scores = jnp.where(k_pos <= q_pos, scores, -1e30)
            old = peak[head]
            fresh = jnp.maximum(old, jnp.max(scores, axis=1, keepdims=True))
            probs = jnp.exp(scores - fresh)
            factor = jnp.exp(old - fresh)
            peak[head] = fresh
            total[head] = total[head] * factor + jnp.sum(probs, axis=1, keepdims=True)
            accum[head] = accum[head] * factor + dot(probs.astype(BF16), values[:, at])

    passed = []
    for j in range(n_seq):
        source_seq = (seq + n_seq - j) % n_seq
        for i in range(n_z):
            slot = source_seq * n_mp + ((z + n_z - i) % n_z) * 2 + core
            if j > 0:
                arrived(slot)
                begin_send(slot, j * n_z + i, 0, (seq, twin))
        for i in range(n_z):
            arrived(source_seq * n_mp + ((z + n_z - i) % n_z) * 2 + 1 - core)
        if j < 2:
            weight_swaps[1 + j].wait_recv()
            passed.append(pass_part(j))
            passed[j].start()
        if j == 0:
            query = dot(block(seq), w_q).astype(BF16)
            attend(query, seq, True)
        else:

            @pl.when(seq >= j)
            def _(j=j):
                attend(query, seq - j, False)

    for head in range(heads):
        at = slice(head * HD, (head + 1) * HD)
        mixed = (accum[head] / total[head]).astype(BF16).reshape(n_z, 2, frames, HD)
        for side in range(2):
            attn_own[side, :, :, at] = mixed[:, side]

    attn_swaps = [swap(3, attn_own.at[1 - core], attn_twin, (seq, twin))]
    for side in range(2):
        attn_swaps.append(
            pltpu.make_async_remote_copy(
                src_ref=attn_own.at[side],
                dst_ref=attn_pair.at[core],
                send_sem=swap_send.at[4 + side],
                recv_sem=swap_recv.at[4 + core],
                device_id=(seq, pair * 2 + side),
                device_id_type=MESH,
            )
        )
    for copy in attn_swaps:
        copy.start()
    loads[5].wait()
    weight_swaps[0].wait_recv()
    for copy in passed:
        copy.wait_recv()
    attn_swaps[0].wait_recv()

    chunks = leaving.shape[1]
    width = leaving.shape[3]
    plain = chunks - paired_width // width

    def whole(ref):
        return ref[...].reshape(n_z * frames, columns)

    def multiply(chunk):
        at = slice(chunk * width, (chunk + 1) * width)
        value = dot(attn_own[core].reshape(n_z * frames, columns), out_own[:, at])
        value = value + dot(whole(attn_twin), out_twin[:, at])
        if chunk >= plain:
            at = slice((chunk - plain) * width, (chunk - plain + 1) * width)
            for side in range(2):
                value = value + dot(whole(attn_pair.at[side]), out_pair[side, :, at])
        leaving[:, chunk] = value.astype(BF16).reshape(n_z, frames, width)

    def hop(way, dest, chunk, device):
        return pltpu.make_async_remote_copy(
            src_ref=leaving.at[dest, chunk],
            dst_ref=coming.at[way, dest, chunk],
            send_sem=chain_send.at[dest, chunk],
            recv_sem=chain_recv.at[way, dest, chunk],
            device_id=(seq, device * 2 + core),
            device_id_type=MESH,
        )

    last = n_z - 1
    odd = z % 2
    near = jnp.where(z < n_z // 2, 0, 1)

    def plan(phase, k, chunk):
        way = near if phase == 0 else 1 - near
        dest = jnp.where(way == 0, n_z - k, k - 1)
        ahead = jnp.where(way == 0, dest - z, z - dest)
        passed_by = jnp.where(way == 0, z, last - z)
        if chunk < plain:
            active, has, stride = ahead > 0, passed_by > 0, 1
        else:
            inner = jnp.where(way == 0, odd, 1 - odd)
            active, has = jnp.logical_and(ahead > 0, inner == 1), passed_by >= 2
            stride = jnp.clip(ahead, 0, 2)
        device = jnp.clip(jnp.where(way == 0, z + stride, z - stride), 0, last)
        return way, dest, active, has, device

    def settle(phase, k, chunk):
        way, dest, active, has, device = plan(phase, k, chunk)

        @pl.when(active)
        def _():
            hop(way, dest, chunk, device).wait_send()

    paired_first = list(range(plain, chunks)) + list(range(plain))
    order = [(p, k, c) for p in range(2) for k in range(1, n_z) for c in paired_first]
    for chunk in range(plain):
        multiply(chunk)
    for side in range(2):
        swap(4 + side, attn_own.at[0], attn_pair.at[side], pair_same).wait_recv()
    for phase, k, chunk in order:
        if phase == 0 and k == 1 and chunk >= plain:
            multiply(chunk)
        way, dest, active, has, device = plan(phase, k, chunk)
        if k > 1:
            settle(phase, k - 1, chunk)

        @pl.when(jnp.logical_and(active, has))
        def _(way=way, dest=dest, chunk=chunk):
            hop(way, dest, chunk, pair).wait_recv()
            leaving[dest, chunk] = (
                leaving[dest, chunk].astype(F32) + coming[way, dest, chunk].astype(F32)
            ).astype(BF16)

        @pl.when(active)
        def _(way=way, dest=dest, chunk=chunk, device=device):
            hop(way, dest, chunk, device).start()

    for chunk in range(chunks):
        at = slice(chunk * width, (chunk + 1) * width)
        frames_sum[:, at] = frames_mine[:, at].astype(F32) + leaving[z, chunk].astype(F32)
        edges = (z > 0, z < last) if chunk < plain else (z >= 2, z < last - 1)
        for way in range(2):

            @pl.when(edges[way])
            def _(way=way, chunk=chunk, at=at):
                hop(way, z, chunk, pair).wait_recv()
                frames_sum[:, at] += coming[way, z, chunk].astype(F32)

        result[:, at] = frames_sum[:, at].astype(BF16)

    edge.wait_send()
    for copy in sent + weight_swaps + passed + attn_swaps:
        copy.wait_send()
    for phase in range(2):
        for chunk in range(chunks):
            settle(phase, last, chunk)


def layer(n_seq, n_mp, audio, first, second, down, proj, gain, qkv, out):
    rows, channels = audio.shape
    frames = rows // STRIDE
    width = proj.shape[1]
    columns = qkv.shape[2]
    heads = columns // HD
    length = frames * n_mp
    n_z = n_mp // 2
    vmem = pl.BlockSpec(memory_space=pltpu.VMEM)
    hbm = pl.BlockSpec(memory_space=pl.ANY)
    flops = 2 * channels * width * columns * 3 + 12 * rows * channels * channels
    return pl.pallas_call(
        functools.partial(layer_kernel, n_seq, n_mp),
        out_shape=jax.ShapeDtypeStruct((frames, width), BF16),
        in_specs=[vmem, hbm, hbm, hbm, hbm, vmem, hbm, hbm],
        out_specs=vmem,
        scratch_shapes=[
            pltpu.VMEM((HALO, channels), BF16),
            pltpu.VMEM(first.shape, BF16),
            pltpu.VMEM(second.shape, BF16),
            pltpu.VMEM(down.shape, BF16),
            pltpu.VMEM(proj.shape, BF16),
            pltpu.VMEM(qkv.shape, BF16),
            pltpu.VMEM((frames + 1, STRIDE, channels), F32),
            pltpu.VMEM((n_seq * n_mp, frames, channels), BF16),
            pltpu.VMEM((3, channels, columns), F32),
            pltpu.VMEM((heads, length, 1), F32),
            pltpu.VMEM((heads, length, 1), F32),
            pltpu.VMEM((heads, length, HD), F32),
            pltpu.VMEM((frames, width), BF16),
            pltpu.VMEM((frames, width), F32),
            pltpu.VMEM(out.shape, BF16),
            pltpu.VMEM(out.shape, BF16),
            pltpu.VMEM((2, columns, width // 2), BF16),
            pltpu.VMEM((2, n_z, frames, columns), BF16),
            pltpu.VMEM((n_z, frames, columns), BF16),
            pltpu.VMEM((2, n_z, frames, columns), BF16),
            pltpu.VMEM((n_z, CHUNKS, frames, width // CHUNKS), BF16),
            pltpu.VMEM((2, n_z, CHUNKS, frames, width // CHUNKS), BF16),
            pltpu.SemaphoreType.DMA((6,)),
            pltpu.SemaphoreType.DMA((2,)),
            pltpu.SemaphoreType.DMA((n_seq * n_z, n_seq + n_z)),
            pltpu.SemaphoreType.DMA((n_seq * n_mp,)),
            pltpu.SemaphoreType.DMA((8,)),
            pltpu.SemaphoreType.DMA((8,)),
            pltpu.SemaphoreType.DMA((n_z, CHUNKS)),
            pltpu.SemaphoreType.DMA((2, n_z, CHUNKS)),
        ],
        compiler_params=pltpu.CompilerParams(
            collective_id=0, has_side_effects=True, vmem_limit_bytes=60 * 2**20
        ),
        cost_estimate=pl.CostEstimate(flops=flops, bytes_accessed=24 * 2**20, transcendentals=0),
    )(audio, first, second, down, proj, gain, qkv, out)


def body(
    n_seq,
    n_mp,
    audio_feats,
    conv_first,
    conv_second,
    down_weight,
    in_proj,
    norm_gain,
    qkv_weight,
    out_weight,
):
    return layer(
        n_seq,
        n_mp,
        audio_feats,
        conv_first,
        conv_second,
        down_weight,
        in_proj,
        norm_gain.reshape(1, -1),
        qkv_weight,
        out_weight,
    )


def solution(mesh):
    placed = (P(("seq", "mp"), None), P(), P(), P(), P(), P(), P(None, None, "mp"), P("mp", None))
    return jax.shard_map(
        functools.partial(body, mesh.shape["seq"], mesh.shape["mp"]),
        mesh=mesh,
        in_specs=placed,
        out_specs=P(("seq", "mp"), None),
        check_vma=False,
    )
```
